32 devices in a mesh: rep: 8 (over z, y), fsdp: 4 (over x, core).
Axes of the slice: x: 2, y: 2, z: 4, core: 2. Of those that a mesh axis runs over, the one named last changes fastest.
Arguments:
- token_ids: int32 [8, 1024], P('rep', 'fsdp'), may hold values from 0 to 128004, as said below
- hidden: bfloat16 [8, 1024, 4096], P('rep', 'fsdp'), may hold values from -600 to 600
- norm_gain: float32 [8, 4096], P('rep'), may hold values from 0.5 to 1.5
- key_weight: bfloat16 [8, 4096, 512], P('rep', 'fsdp'), may hold values from -0.09375 to 0.09375
- key_cot: bfloat16 [8, 1024, 512], P('rep', 'fsdp'), may hold values from -0.119628906 to 0.119628906
- frag_base: float32 [4096, 512], P('fsdp'), may hold values from -3 to 3
- frag_local: bfloat16 [8, 4096, 512], P('rep', 'fsdp'), may hold values from -16 to 16
- momentum: bfloat16 [4096, 512], P('fsdp'), may hold values from -1.796875 to 1.796875
Outputs:
- keys: bfloat16 [8, 1024, 512], P('rep', 'fsdp')
- weight_grad: bfloat16 [8, 4096, 512], P('rep', 'fsdp')
- gain_grad: float32 [8, 4096], P('rep')
- new_params: float32 [4096, 512], P('fsdp')
- new_momentum: bfloat16 [4096, 512], P('fsdp')
The draws below stay inside these ranges and needn't reach their ends.
Inputs may be any that keep to these rules, and one draw needn't show every extreme that they name: `token_ids`: each aligned sequence of 64 ids holds between 16 and 63 ordinary ids, each below 128000, followed by the padding id 128004 up to its end.
All inputs are finite; a program needn't handle non-finite values.
Results may differ from the reference program's by a relative error of at most 0.009.
Values may be sent and summed in bfloat16 or wider, within the bound.
A program may use at most 128 MiB of HBM per device.

```python
import math
import jax
import jax.numpy as jnp
from jax import lax

D = 4096
LEN = 64
TOK_DEV = 256
KW = 512
TOK_REP = 1024
REPS = 8
N_FSDP = 4


def fragment_base(key):
    return 0.5 * jnp.clip(jax.random.normal(key, (D, KW), jnp.float32), -6.0, 6.0)


def draw_token_ids(key, part):
    key = jax.random.fold_in(key, 2)
    key_len, key_tok = jax.random.split(key)
    seq_count = REPS * TOK_REP // LEN
    lengths = jax.random.randint(key_len, (seq_count, 1), LEN // 4, LEN)
    drawn = jax.random.randint(key_tok, (seq_count, LEN), 0, 128000)
    position = jnp.arange(LEN)[None, :]
    tokens = jnp.where(position < lengths, drawn, 128004)
    return tokens.reshape(REPS, TOK_REP).astype(jnp.int32)


def draw_hidden(key, part):
    key = jax.random.fold_in(key, 4)
    key_row, key_col, key_val = jax.random.split(key, 3)
    row_scale = jnp.exp(jax.random.uniform(key_row, (REPS, TOK_REP, 1), jnp.float32) * math.log(10.0))
    col_scale = jnp.exp(jax.random.uniform(key_col, (1, 1, D), jnp.float32) * math.log(10.0))
    values = jnp.clip(jax.random.normal(key_val, (REPS, TOK_REP, D), jnp.float32), -6.0, 6.0)
    return (values * row_scale * col_scale).astype(jnp.bfloat16)


def draw_frag_base(key, part):
    shared = fragment_base(key)
    return shared


def draw_frag_local(key, part):
    shared = fragment_base(key)
    key = jax.random.fold_in(key, 5)
    key_row, key_col, key_val = jax.random.split(key, 3)
    row_scale = jnp.exp(jax.random.uniform(key_row, (REPS, D, 1), jnp.float32) * math.log(10.0))
    col_scale = jnp.exp(jax.random.uniform(key_col, (REPS, 1, KW), jnp.float32) * math.log(10.0))
    noise = jnp.clip(jax.random.normal(key_val, (REPS, D, KW), jnp.float32), -6.0, 6.0)
    return (shared[None] - 0.01 * row_scale * col_scale * noise).astype(jnp.bfloat16)


def shard_levels(key, extent, pieces, smallest, high):
    def one(dim, shards_of):
        steps = jax.random.uniform(jax.random.fold_in(jax.random.fold_in(key, 6), dim), (shards_of,), jnp.float32, smallest / len(pieces), high / len(pieces))
        return jnp.repeat(jnp.exp(steps), extent[dim] // shards_of).reshape((-1,) + (1,) * (len(extent) - dim - 1))

    level = one(*pieces[0])
    for cut in pieces[1:]:
        level = level * one(*cut)
    return level


def centred(own_key, shape, scale, reach, cuts=(), kind=jnp.bfloat16):
    entries = scale * jax.random.normal(own_key, shape, jnp.float32)
    if cuts:
        entries = entries * shard_levels(own_key, shape, cuts, -0.22, 0.18)
    return jnp.clip(entries, -reach, reach).astype(kind)


def setup_inputs(seed: int = 0) -> dict:
    streams_of = jax.random.split(jax.random.key(seed), 9)
    return {
        "token_ids": draw_token_ids(jax.random.fold_in(streams_of[8], 71), 0),
        "hidden": draw_hidden(jax.random.fold_in(streams_of[8], 71), 0),
        "norm_gain": jnp.clip(1.0 + 0.1 * jax.random.normal(streams_of[2], (REPS, D), jnp.float32), 0.5, 1.5),
        "key_weight": centred(streams_of[3], (REPS, D, KW), D ** -0.5, 0.09375, ((0, 8), (1, 4))),
        "key_cot": centred(streams_of[4], (REPS, TOK_REP, KW), 0.02, 0.119628906, ((0, 8), (1, 4))),
        "frag_base": draw_frag_base(jax.random.fold_in(streams_of[8], 71), 0),
        "frag_local": draw_frag_local(jax.random.fold_in(streams_of[8], 71), 0),
        "momentum": centred(streams_of[7], (D, KW), 0.3, 1.796875, ((0, 4),)),
    }


pad_token = 128004
norm_eps = 1e-05
nesterov_mu = 0.9
outer_rate = 0.7

def loss_weights(token_ids):
    grouped = token_ids.reshape(token_ids.shape[0], -1, LEN)
    is_live = (grouped != pad_token).astype(jnp.float32)
    live_count = lax.optimization_barrier(jnp.sum(is_live, -1, keepdims=True))
    return (LEN * is_live / live_count).reshape(token_ids.shape[0], -1)

def inner_one(operands):
    hidden, gain, weight, key_cot, loss_weight = operands
    x_float = hidden.astype(jnp.float32)
    inv_rms = lax.rsqrt(lax.optimization_barrier(jnp.mean(x_float * x_float, -1, keepdims=True)) + norm_eps)
    scaled = x_float * inv_rms
    normed = (scaled * gain).astype(jnp.bfloat16)
    keys = jnp.dot(normed, weight, preferred_element_type=jnp.float32).astype(jnp.bfloat16)
    weighted = (loss_weight[:, None] * key_cot.astype(jnp.float32)).astype(jnp.bfloat16)
    grouped_h = normed.reshape(N_FSDP, TOK_DEV, -1).astype(jnp.float32)
    grouped_e = weighted.reshape(N_FSDP, TOK_DEV, -1).astype(jnp.float32)
    partials = jnp.einsum('gtd,gtk->gdk', grouped_h, grouped_e)
    rounded = lax.optimization_barrier(partials.astype(jnp.bfloat16)).astype(jnp.float32)
    weight_grad = lax.optimization_barrier(jnp.sum(rounded, 0)).astype(jnp.bfloat16)
    normed_grad = lax.dot_general(weighted, weight, (((1,), (1,)), ((), ())), preferred_element_type=jnp.float32)
    gain_grad = lax.optimization_barrier(jnp.sum(normed_grad * scaled, 0))
    return (keys, weight_grad, gain_grad)

def reference(token_ids, hidden, norm_gain, key_weight, key_cot, frag_base, frag_local, momentum):
    loss_weight = loss_weights(token_ids)
    keys, weight_grad, gain_grad = lax.map(inner_one, (hidden, norm_gain, key_weight, key_cot, loss_weight))
    pseudo_grad = (frag_base[None] - frag_local.astype(jnp.float32)).astype(jnp.bfloat16)
    outer_grad = lax.optimization_barrier(jnp.sum(pseudo_grad.astype(jnp.float32), 0)) / REPS
    momentum_next = nesterov_mu * momentum.astype(jnp.float32) + outer_grad
    new_params = frag_base - outer_rate * (nesterov_mu * momentum_next + outer_grad)
    return (keys, weight_grad, gain_grad, new_params, momentum_next.astype(jnp.bfloat16))
```

```python
import functools

import jax
import jax.numpy as jnp
from jax import lax
from jax.experimental import pallas as pl
from jax.experimental.pallas import tpu as pltpu
from jax.sharding import PartitionSpec as P

LEN = 64
LANES = 128
CORES = 2
PAIR = 2
CHUNKS = 4

pad_token = 128004
norm_eps = 1e-05
nesterov_mu = 0.9
outer_rate = 0.7

MESH = pl.DeviceIdType.MESH


class Counter:
    def __init__(self):
        self.n = 0

    def take(self, count=1):
        first = self.n
        self.n += count
        return first


def semaphore_plan(nf, nr):
    chips, outer = nf // CORES, nr // PAIR
    c = Counter()
    plan = {
        "w": c.take(),
        "sib": c.take(),
        "wt_sib": c.take(),
        "wt": c.take(chips),
        "wt_fwd": c.take(chips),
        "nrm": c.take(chips * CHUNKS),
        "fwd": c.take(chips * CHUNKS),
        "kp": c.take(chips * CHUNKS),
        "gain": c.take(nf),
        "y": c.take(2),
        "z": c.take(2 * outer),
        "zag": c.take(2 * outer),
        "yag": c.take(2),
    }
    return plan, c.n


def transposed_dot(a, b):
    return lax.dot_general(a, b, (((0,), (0,)), ((), ())), preferred_element_type=jnp.float32)


def kernel(
    nf, nr, plan,
    ids_h, hid_h, gain_h, w_h, cot_h, base_h, loc_h,
    keys_h, wgrad_h, ggrad_h, outer_h,
    ids, hid, gain, wch, cot, base, loc,
    nrm, rn, sn, fn, wt, wt_s, wt_p, wt_f, pk, kp, kacc, kout,
    grad, wout, gg, gout,
    ps, yr, ys, zr, og,
    ss, rs, ls,
):
    tok = hid.shape[0]
    dn = base.shape[0]
    chips, outer = nf // CORES, nr // PAIR
    zrows = dn // outer
    ct = tok // CHUNKS
    f = lax.axis_index("fsdp")
    r = lax.axis_index("rep")
    x, c = lax.div(f, CORES), lax.rem(f, CORES)
    sib = f + 1 - 2 * c
    z, h = lax.div(r, PAIR), lax.rem(r, PAIR)
    partner = r + 1 - 2 * h

    def chip_at(j):
        return lax.rem(x + j, chips)

    def z_at(j):
        return lax.rem(z + j, outer)

    def local(i, src, dst):
        copy = pltpu.make_async_copy(src, dst, ls.at[i])
        copy.start()
        return copy

    l_cot = local(0, cot_h.at[0], cot)
    l_ids = local(1, ids_h, ids)
    l_gain = local(2, gain_h, gain)
    l_hid = local(3, hid_h.at[0], hid)
    l_w = local(4, w_h.at[0], wch.at[c])
    l_base = local(5, base_h, base)
    l_loc = local(6, loc_h.at[0], loc)

    barrier = pltpu.get_barrier_semaphore()
    greeted = 0
    for o in range(1, nf):
        pl.semaphore_signal(barrier, inc=1, device_id={"fsdp": lax.rem(f + o, nf)}, device_id_type=MESH)
        greeted += 1
    pl.semaphore_signal(barrier, inc=1, device_id={"rep": partner}, device_id_type=MESH)
    greeted += 1
    for o in range(1, outer):
        pl.semaphore_signal(barrier, inc=1, device_id={"rep": z_at(o) * PAIR + h}, device_id_type=MESH)
        greeted += 1

    sent = []

    def copy_of(src, dst, sid, rid, dev):
        return pltpu.make_async_remote_copy(
            src_ref=src, dst_ref=dst, send_sem=ss.at[sid], recv_sem=rs.at[rid],
            device_id=dev, device_id_type=MESH,
        )

    def send(src, dst, sid, rid, dev):
        copy = copy_of(src, dst, sid, rid, dev)
        copy.start()
        sent.append(copy)

    def arrived(dst, rid):
        copy_of(dst, dst, rid, rid, {"fsdp": sib}).wait_recv()

    l_ids.wait()
    row = lax.broadcasted_iota(jnp.int32, (tok, tok), 0)
    col = lax.broadcasted_iota(jnp.int32, (tok, tok), 1)
    live = jnp.where(ids[...] != pad_token, 1.0, 0.0).astype(jnp.float32)
    live = jnp.broadcast_to(live, (tok, tok))
    count = jnp.sum(jnp.where(lax.div(row, LEN) == lax.div(col, LEN), live, 0.0), -1, keepdims=True)
    own = jnp.sum(jnp.where(row == col, live, 0.0), -1, keepdims=True)
    loss_weight = LEN * own / count
    l_cot.wait()
    wt[...] = (loss_weight * cot[...].astype(jnp.float32)).astype(jnp.bfloat16)

    pl.semaphore_wait(barrier, greeted)

    def peer(j):
        return {"fsdp": chip_at(j) * CORES + c}

    for j in range(1, chips):
        send(wt, wt_p.at[chips - j], plan["wt"] + j, plan["wt"] + chips - j, peer(j))
    send(wt, wt_s, plan["wt_sib"], plan["wt_sib"], {"fsdp": sib})
    send(w_h.at[0], wch.at[c], plan["w"], plan["w"], {"fsdp": sib})

    l_gain.wait()
    l_hid.wait()
    sub = 16

    def norm_rows(i, carry):
        rows = pl.ds(pl.multiple_of(i * sub, sub), sub)
        v = hid[rows, :].astype(jnp.float32)
        inv = lax.rsqrt(jnp.mean(v * v, -1, keepdims=True) + norm_eps)
        for d in range(nf):
            part = hid[rows, d * dn:(d + 1) * dn].astype(jnp.float32)
            nrm[d, rows, :] = (part * inv * gain[:, d * dn:(d + 1) * dn]).astype(jnp.bfloat16)
        return carry

    for q in range(CHUNKS):
        lax.fori_loop(q * (ct // sub), (q + 1) * (ct // sub), norm_rows, 0)
        rows = pl.ds(q * ct, ct)
        for j in range(1, chips):
            send(
                nrm.at[pl.ds(chip_at(j) * CORES, CORES), rows, :],
                rn.at[chips - j, :, rows, :],
                plan["nrm"] + j * CHUNKS + q,
                plan["nrm"] + (chips - j) * CHUNKS + q,
                peer(j),
            )
    send(nrm.at[sib], sn, plan["sib"], plan["sib"], {"fsdp": sib})

    l_base.wait()
    l_loc.wait()
    step = 64

    def pseudo_rows(i, carry):
        rows = pl.ds(pl.multiple_of(i * step, step), step)
        for g in range(4):
            cols = slice(g * LANES, (g + 1) * LANES)
            ps[g, rows, :] = (base[rows, cols] - loc[rows, cols].astype(jnp.float32)).astype(jnp.bfloat16)
        return carry

    lax.fori_loop(0, dn // step, pseudo_rows, 0)
    for k in range(2):
        send(ps.at[2 * (1 - h) + k], yr.at[k], plan["y"] + k, plan["y"] + k, {"rep": partner})

    l_w.wait()
    arrived(wch.at[1 - c], plan["w"])
    kacc[...] = jnp.dot(nrm[2 * x], wch[0], preferred_element_type=jnp.float32)
    kacc[...] += jnp.dot(nrm[2 * x + 1], wch[1], preferred_element_type=jnp.float32)

    tile = min(256, dn)

    def grad_tiles(rows_of, tokens_of, first):
        for i in range(dn // tile):
            cut = slice(i * tile, (i + 1) * tile)
            term = transposed_dot(rows_of(cut), tokens_of[...])
            if first:
                grad[cut, :] = term
            else:
                grad[cut, :] += term

    grad_tiles(lambda cut: nrm[f, :, cut], wt, True)
    arrived(wt_s, plan["wt_sib"])
    arrived(sn, plan["sib"])
    grad_tiles(lambda cut: sn[:, cut], wt_s, False)

    for j in range(1, chips):
        arrived(wt_p.at[j], plan["wt"] + j)
        send(wt_p.at[j], wt_f.at[j], plan["wt_fwd"] + j, plan["wt_fwd"] + j, {"fsdp": sib})

    def peer_chunk(q):
        rows = pl.ds(q * ct, ct)
        for j in range(1, chips):
            arrived(rn.at[j, :, rows, :], plan["nrm"] + j * CHUNKS + q)
            send(
                rn.at[j, 1 - c, rows, :], fn.at[j, rows, :],
                plan["fwd"] + j * CHUNKS + q, plan["fwd"] + j * CHUNKS + q, {"fsdp": sib},
            )
            part = jnp.dot(rn[j, 0, rows, :], wch[0], preferred_element_type=jnp.float32)
            part += jnp.dot(rn[j, 1, rows, :], wch[1], preferred_element_type=jnp.float32)
            pk[j, rows, :] = part.astype(jnp.bfloat16)
            send(
                pk.at[j, rows, :], kp.at[chips - j, rows, :],
                plan["kp"] + j * CHUNKS + q, plan["kp"] + (chips - j) * CHUNKS + q, peer(j),
            )

    def pair_sum(k):
        arrived(yr.at[k], plan["y"] + k)
        ys[k] = (ps[2 * h + k].astype(jnp.float32) + yr[k].astype(jnp.float32)).astype(jnp.bfloat16)
        for o in range(1, outer):
            send(
                ys.at[k, pl.ds(pl.multiple_of(z_at(o) * zrows, 16), zrows), :],
                zr.at[k, outer - o],
                plan["z"] + k * outer + o, plan["z"] + k * outer + outer - o,
                {"rep": z_at(o) * PAIR + h},
            )

    mine = pl.ds(pl.multiple_of(z * zrows, 16), zrows)

    def outer_sum(k):
        total = ys[k, mine, :].astype(jnp.float32)
        for o in range(1, outer):
            arrived(zr.at[k, o], plan["z"] + k * outer + o)
            total += zr[k, o].astype(jnp.float32)
        og[2 * h + k, mine, :] = total.astype(jnp.bfloat16)
        for o in range(1, outer):
            send(
                og.at[2 * h + k, mine, :], og.at[2 * h + k, mine, :],
                plan["zag"] + k * outer + o, plan["zag"] + k * outer + outer - o,
                {"rep": z_at(o) * PAIR + h},
            )

    def outer_back(k):
        for o in range(1, outer):
            there = pl.ds(pl.multiple_of(z_at(o) * zrows, 16), zrows)
            arrived(og.at[2 * h + k, there, :], plan["zag"] + k * outer + o)
        send(og.at[2 * h + k], og.at[2 * h + k], plan["yag"] + k, plan["yag"] + k, {"rep": partner})

    peer_chunk(0)
    pair_sum(0)
    peer_chunk(1)
    pair_sum(1)
    outer_sum(0)
    peer_chunk(2)
    outer_sum(1)
    outer_back(0)
    peer_chunk(3)
    outer_back(1)

    for j in range(1, chips):
        grad_tiles(lambda cut: rn[j, c, :, cut], wt_p.at[j], False)
        arrived(wt_f.at[j], plan["wt_fwd"] + j)
        for q in range(CHUNKS):
            arrived(fn.at[j, pl.ds(q * ct, ct), :], plan["fwd"] + j * CHUNKS + q)
        grad_tiles(lambda cut: fn[j, :, cut], wt_f.at[j], False)

    ones = jnp.ones((8, wout.shape[1]), jnp.bfloat16)
    nt = (((1,), (1,)), ((), ()))
    for i in range(dn // tile):
        cut = slice(i * tile, (i + 1) * tile)
        g = grad[cut, :]
        wout[cut, :] = g.astype(jnp.bfloat16)
        prod = g * wch[c, cut, :].astype(jnp.float32)
        hi = prod.astype(jnp.bfloat16)
        lo = (prod - hi.astype(jnp.float32)).astype(jnp.bfloat16)
        sums = lax.dot_general(ones, hi, nt, preferred_element_type=jnp.float32)
        sums += lax.dot_general(ones, lo, nt, preferred_element_type=jnp.float32)
        gcols = pl.ds(pl.multiple_of(f * dn + i * tile, LANES), tile)
        gg[f, :, cut] = sums / gain[:, gcols]
    for o in range(1, nf):
        send(gg.at[f], gg.at[f], plan["gain"] + o, plan["gain"] + nf - o, {"fsdp": lax.rem(f + o, nf)})
    l_wout = local(7, wout, wgrad_h.at[0])

    for j in range(1, chips):
        for q in range(CHUNKS):
            rows = pl.ds(q * ct, ct)
            arrived(kp.at[j, rows, :], plan["kp"] + j * CHUNKS + q)
        kacc[...] += kp[j].astype(jnp.float32)
    kout[...] = kacc[...].astype(jnp.bfloat16)
    l_kout = local(8, kout, keys_h.at[0])

    for k in range(2):
        arrived(og.at[2 * (1 - h) + k], plan["yag"] + k)
    l_og = [local(10 + g, og.at[g], outer_h.at[:, pl.ds(g * LANES, LANES)]) for g in range(4)]

    for o in range(1, nf):
        arrived(gg.at[lax.rem(f + o, nf)], plan["gain"] + o)
    for d in range(nf):
        gout[:, d * dn:(d + 1) * dn] = gg[d, 0:1, :]
    l_gout = local(9, gout, ggrad_h)

    for copy in sent:
        copy.wait_send()
    for copy in [l_wout, l_kout, l_gout] + l_og:
        copy.wait()


def exchange(nf, nr, token_ids, hidden, norm_gain, key_weight, key_cot, frag_base, frag_local):
    tok, d = hidden.shape[1:]
    dn, kw = frag_base.shape
    chips, outer = nf // CORES, nr // PAIR
    plan, n_sem = semaphore_plan(nf, nr)
    bf, f32 = jnp.bfloat16, jnp.float32
    vmem = pltpu.VMEM
    anyspace = pl.BlockSpec(memory_space=pl.ANY)
    scratch = [
        vmem((1, tok), jnp.int32), vmem((tok, d), bf), vmem((1, d), f32), vmem((CORES, dn, kw), bf),
        vmem((tok, kw), bf), vmem((dn, kw), f32), vmem((dn, kw), bf),
        vmem((nf, tok, dn), bf), vmem((chips, CORES, tok, dn), bf), vmem((tok, dn), bf),
        vmem((chips, tok, dn), bf),
        vmem((tok, kw), bf), vmem((tok, kw), bf), vmem((chips, tok, kw), bf), vmem((chips, tok, kw), bf),
        vmem((chips, tok, kw), bf), vmem((chips, tok, kw), bf), vmem((tok, kw), f32), vmem((tok, kw), bf),
        vmem((dn, kw), f32), vmem((dn, kw), bf), vmem((nf, 8, dn), f32), vmem((1, d), f32),
        vmem((4, dn, LANES), bf), vmem((2, dn, LANES), bf), vmem((2, dn, LANES), bf),
        vmem((2, outer, dn // outer, LANES), bf), vmem((4, dn, LANES), bf),
        pltpu.SemaphoreType.DMA((n_sem,)), pltpu.SemaphoreType.DMA((n_sem,)), pltpu.SemaphoreType.DMA((14,)),
    ]
    return pl.pallas_call(
        functools.partial(kernel, nf, nr, plan),
        out_shape=(
            jax.ShapeDtypeStruct((1, tok, kw), bf),
            jax.ShapeDtypeStruct((1, dn, kw), bf),
            jax.ShapeDtypeStruct((1, d), f32),
            jax.ShapeDtypeStruct((dn, kw), bf),
        ),
        in_specs=[anyspace] * 7,
        out_specs=(anyspace,) * 4,
        scratch_shapes=scratch,
        compiler_params=pltpu.CompilerParams(
            collective_id=0, has_side_effects=True, vmem_limit_bytes=56 * 1024 * 1024
        ),
    )(token_ids, hidden, norm_gain, key_weight, key_cot, frag_base, frag_local)


def body(nf, nr, token_ids, hidden, norm_gain, key_weight, key_cot, frag_base, frag_local, momentum):
    keys, weight_grad, gain_grad, total = exchange(
        nf, nr, token_ids, hidden, norm_gain, key_weight, key_cot, frag_base, frag_local
    )
    outer_grad = total.astype(jnp.float32) / nr
    momentum_next = nesterov_mu * momentum.astype(jnp.float32) + outer_grad
    new_params = frag_base - outer_rate * (nesterov_mu * momentum_next + outer_grad)
    return (keys, weight_grad, gain_grad, new_params, momentum_next.astype(jnp.bfloat16))


def solution(mesh):
    return jax.shard_map(
        functools.partial(body, mesh.shape["fsdp"], mesh.shape["rep"]),
        mesh=mesh,
        in_specs=(
            P("rep", "fsdp"),
            P("rep", "fsdp", None),
            P("rep", None),
            P("rep", "fsdp", None),
            P("rep", "fsdp", None),
            P("fsdp", None),
            P("rep", "fsdp", None),
            P("fsdp", None),
        ),
        out_specs=(
            P("rep", "fsdp", None),
            P("rep", "fsdp", None),
            P("rep", None),
            P("fsdp", None),
            P("fsdp", None),
        ),
        check_vma=False,
    )
```

```python
import functools

import jax
import jax.numpy as jnp
from jax import lax
from jax.experimental import pallas as pl
from jax.experimental.pallas import tpu as pltpu
from jax.sharding import PartitionSpec as P

LEN = 64
LANES = 128
CORES = 2
PAIR = 2
CHUNKS = 4

pad_token = 128004
norm_eps = 1e-05
nesterov_mu = 0.9
outer_rate = 0.7

MESH = pl.DeviceIdType.MESH


class Counter:
    def __init__(self):
        self.n = 0

    def take(self, count=1):
        first = self.n
        self.n += count
        return first


def semaphore_plan(nf, nr, pieces):
    chips, outer = nf // CORES, nr // PAIR
    c = Counter()
    plan = {
        "w": c.take(),
        "sib": c.take(),
        "wt_sib": c.take(),
        "wt": c.take(chips),
        "wt_fwd": c.take(chips),
        "nrm": c.take(chips * CHUNKS),
        "fwd": c.take(chips * CHUNKS),
        "kp": c.take(chips * CHUNKS),
        "gain": c.take(nf),
        "y": c.take(pieces),
        "z": c.take(pieces * outer),
        "zag": c.take(pieces * outer),
        "yag": c.take(pieces),
    }
    return plan, c.n


def transposed_dot(a, b):
    return lax.dot_general(a, b, (((0,), (0,)), ((), ())), preferred_element_type=jnp.float32)


def kernel(
    nf, nr, pieces, plan,
    ids_h, hid_h, gain_h, w_h, cot_h, base_h, loc_h,
    keys_h, wgrad_h, ggrad_h, outer_h,
    ids, hid, gain, wch, cot, base, loc,
    nrm, rn, sn, fn, wt, wt_s, wt_p, wt_f, pk, kp, kacc, kout,
    grad, wout, gg, gout,
    ps, yr, ys, zr, og,
    ss, rs, ls,
):
    tok = hid.shape[0]
    dn = base.shape[0]
    chips, outer = nf // CORES, nr // PAIR
    width = base.shape[1] // PAIR
    groups = width // LANES
    prows = dn * groups // pieces
    zrows = prows // outer
    ct = tok // CHUNKS
    f = lax.axis_index("fsdp")
    r = lax.axis_index("rep")
    x, c = lax.div(f, CORES), lax.rem(f, CORES)
    sib = f + 1 - 2 * c
    z, h = lax.div(r, PAIR), lax.rem(r, PAIR)
    partner = r + 1 - 2 * h

    def chip_at(j):
        return lax.rem(x + j, chips)

    def z_at(j):
        return lax.rem(z + j, outer)

    def local(i, src, dst):
        copy = pltpu.make_async_copy(src, dst, ls.at[i])
        copy.start()
        return copy

    l_cot = local(0, cot_h.at[0], cot)
    l_ids = local(1, ids_h, ids)
    l_gain = local(2, gain_h, gain)
    l_hid = local(3, hid_h.at[0], hid)
    l_w = local(4, w_h.at[0], wch.at[c])
    l_base = local(5, base_h, base)
    l_loc = local(6, loc_h.at[0], loc)

    barrier = pltpu.get_barrier_semaphore()
    greeted = 0
    for o in range(1, nf):
        pl.semaphore_signal(barrier, inc=1, device_id={"fsdp": lax.rem(f + o, nf)}, device_id_type=MESH)
        greeted += 1
    pl.semaphore_signal(barrier, inc=1, device_id={"rep": partner}, device_id_type=MESH)
    greeted += 1
    for o in range(1, outer):
        pl.semaphore_signal(barrier, inc=1, device_id={"rep": z_at(o) * PAIR + h}, device_id_type=MESH)
        greeted += 1

    sent = []

    def copy_of(src, dst, sid, rid, dev):
        return pltpu.make_async_remote_copy(
            src_ref=src, dst_ref=dst, send_sem=ss.at[sid], recv_sem=rs.at[rid],
            device_id=dev, device_id_type=MESH,
        )

    def send(src, dst, sid, rid, dev):
        copy = copy_of(src, dst, sid, rid, dev)
        copy.start()
        sent.append(copy)

    def arrived(dst, rid):
        copy_of(dst, dst, rid, rid, {"fsdp": sib}).wait_recv()

    def peer(j):
        return {"fsdp": chip_at(j) * CORES + c}

    step = min(64, prows)

    def pseudo(half, k, rows):
        g, b = k % groups, k // groups
        cols = pl.ds(pl.multiple_of(half * width + g * LANES, LANES), LANES)
        rows = pl.ds(pl.multiple_of(b * prows + rows * step, step), step)
        return (base[rows, cols] - loc[rows, cols].astype(jnp.float32)).astype(jnp.bfloat16)

    def pseudo_rows(k, i, carry):
        ps[k, pl.ds(pl.multiple_of(i * step, step), step), :] = pseudo(1 - h, k, i)
        return carry

    l_base.wait()
    l_loc.wait()
    for k in range(pieces):
        lax.fori_loop(0, prows // step, functools.partial(pseudo_rows, k), 0)
        if k == 0:
            pl.semaphore_wait(barrier, greeted)
        send(ps.at[k], yr.at[k], plan["y"] + k, plan["y"] + k, {"rep": partner})

    l_ids.wait()
    row = lax.broadcasted_iota(jnp.int32, (tok, tok), 0)
    col = lax.broadcasted_iota(jnp.int32, (tok, tok), 1)
    live = jnp.where(ids[...] != pad_token, 1.0, 0.0).astype(jnp.float32)
    live = jnp.broadcast_to(live, (tok, tok))
    count = jnp.sum(jnp.where(lax.div(row, LEN) == lax.div(col, LEN), live, 0.0), -1, keepdims=True)
    own = jnp.sum(jnp.where(row == col, live, 0.0), -1, keepdims=True)
    loss_weight = LEN * own / count
    l_cot.wait()
    wt[...] = (loss_weight * cot[...].astype(jnp.float32)).astype(jnp.bfloat16)

    l_gain.wait()
    l_hid.wait()
    sub = 16

    def norm_rows(i, carry):
        rows = pl.ds(pl.multiple_of(i * sub, sub), sub)
        v = hid[rows, :].astype(jnp.float32)
        inv = lax.rsqrt(jnp.mean(v * v, -1, keepdims=True) + norm_eps)
        for d in range(nf):
            part = hid[rows, d * dn:(d + 1) * dn].astype(jnp.float32)
            nrm[d, rows, :] = (part * inv * gain[:, d * dn:(d + 1) * dn]).astype(jnp.bfloat16)
        return carry

    for q in range(CHUNKS):
        if q == 1:
            send(w_h.at[0], wch.at[c], plan["w"], plan["w"], {"fsdp": sib})
            for j in range(1, chips):
                send(wt, wt_p.at[chips - j], plan["wt"] + j, plan["wt"] + chips - j, peer(j))
            send(wt, wt_s, plan["wt_sib"], plan["wt_sib"], {"fsdp": sib})
        lax.fori_loop(q * (ct // sub), (q + 1) * (ct // sub), norm_rows, 0)
        rows = pl.ds(q * ct, ct)
        for j in range(1, chips):
            send(
                nrm.at[pl.ds(chip_at(j) * CORES, CORES), rows, :],
                rn.at[chips - j, :, rows, :],
                plan["nrm"] + j * CHUNKS + q,
                plan["nrm"] + (chips - j) * CHUNKS + q,
                peer(j),
            )
    send(nrm.at[sib], sn, plan["sib"], plan["sib"], {"fsdp": sib})

    tile = min(256, dn)

    def grad_tiles(rows_of, tokens_of, first):
        for i in range(dn // tile):
            cut = slice(i * tile, (i + 1) * tile)
            term = transposed_dot(rows_of(cut), tokens_of[...])
            if first:
                grad[cut, :] = term
            else:
                grad[cut, :] += term

    def peer_chunk(q):
        rows = pl.ds(q * ct, ct)
        for j in range(1, chips):
            if q == 0:
                arrived(wt_p.at[j], plan["wt"] + j)
                send(wt_p.at[j], wt_f.at[j], plan["wt_fwd"] + j, plan["wt_fwd"] + j, {"fsdp": sib})
            arrived(rn.at[j, :, rows, :], plan["nrm"] + j * CHUNKS + q)
            send(
                rn.at[j, 1 - c, rows, :], fn.at[j, rows, :],
                plan["fwd"] + j * CHUNKS + q, plan["fwd"] + j * CHUNKS + q, {"fsdp": sib},
            )
            part = jnp.dot(rn[j, 0, rows, :], wch[0], preferred_element_type=jnp.float32)
            part += jnp.dot(rn[j, 1, rows, :], wch[1], preferred_element_type=jnp.float32)
            pk[j, rows, :] = part.astype(jnp.bfloat16)
            send(
                pk.at[j, rows, :], kp.at[chips - j, rows, :],
                plan["kp"] + j * CHUNKS + q, plan["kp"] + (chips - j) * CHUNKS + q, peer(j),
            )

    def own_keys(half):
        n = tok // 2
        rows = slice(half * n, (half + 1) * n)
        kacc[rows, :] = jnp.dot(nrm[2 * x, rows, :], wch[0], preferred_element_type=jnp.float32)
        kacc[rows, :] += jnp.dot(nrm[2 * x + 1, rows, :], wch[1], preferred_element_type=jnp.float32)

    def pair_sum(k):
        arrived(yr.at[k], plan["y"] + k)

        def some(i, carry):
            rows = pl.ds(pl.multiple_of(i * step, step), step)
            total = pseudo(h, k, i).astype(jnp.float32) + yr[k, rows, :].astype(jnp.float32)
            ys[k, rows, :] = total.astype(jnp.bfloat16)
            return carry

        lax.fori_loop(0, prows // step, some, 0)
        for o in range(1, outer):
            send(
                ys.at[k, pl.ds(pl.multiple_of(z_at(o) * zrows, 16), zrows), :],
                zr.at[k, outer - o],
                plan["z"] + k * outer + o, plan["z"] + k * outer + outer - o,
                {"rep": z_at(o) * PAIR + h},
            )

    mine = pl.ds(pl.multiple_of(z * zrows, 16), zrows)

    def outer_sum(k):
        total = ys[k, mine, :].astype(jnp.float32)
        for o in range(1, outer):
            arrived(zr.at[k, o], plan["z"] + k * outer + o)
            total += zr[k, o].astype(jnp.float32)
        og[h, k, mine, :] = total.astype(jnp.bfloat16)
        for o in range(1, outer):
            send(
                og.at[h, k, mine, :], og.at[h, k, mine, :],
                plan["zag"] + k * outer + o, plan["zag"] + k * outer + outer - o,
                {"rep": z_at(o) * PAIR + h},
            )

    def outer_out(half, k):
        g, b = k % groups, k // groups
        cols = pl.ds(pl.multiple_of(half * width + g * LANES, LANES), LANES)
        return og.at[half, k], outer_h.at[pl.ds(b * prows, prows), cols]

    l_og = []

    def outer_back(k):
        for o in range(1, outer):
            there = pl.ds(pl.multiple_of(z_at(o) * zrows, 16), zrows)
            arrived(og.at[h, k, there, :], plan["zag"] + k * outer + o)
        send(og.at[h, k], og.at[h, k], plan["yag"] + k, plan["yag"] + k, {"rep": partner})
        l_og.append(local(10 + k, *outer_out(h, k)))

    def if_piece(step_of, k):
        if k < pieces:
            step_of(k)

    pair_sum(0)
    pair_sum(1)
    l_w.wait()
    arrived(wch.at[1 - c], plan["w"])
    own_keys(0)
    if_piece(pair_sum, 2)
    outer_sum(0)
    if_piece(pair_sum, 3)
    outer_sum(1)
    peer_chunk(0)
    outer_back(0)
    if_piece(outer_sum, 2)
    own_keys(1)
    outer_back(1)
    if_piece(outer_sum, 3)
    peer_chunk(1)
    if_piece(outer_back, 2)
    grad_tiles(lambda cut: nrm[f, :, cut], wt, True)
    if_piece(outer_back, 3)
    peer_chunk(2)
    arrived(wt_s, plan["wt_sib"])
    arrived(sn, plan["sib"])
    grad_tiles(lambda cut: sn[:, cut], wt_s, False)
    peer_chunk(3)

    for j in range(1, chips):
        grad_tiles(lambda cut: rn[j, c, :, cut], wt_p.at[j], False)
        arrived(wt_f.at[j], plan["wt_fwd"] + j)
        for q in range(CHUNKS):
            arrived(fn.at[j, pl.ds(q * ct, ct), :], plan["fwd"] + j * CHUNKS + q)
        grad_tiles(lambda cut: fn[j, :, cut], wt_f.at[j], False)

    ones = jnp.ones((8, wout.shape[1]), jnp.bfloat16)
    nt = (((1,), (1,)), ((), ()))
    for i in range(dn // tile):
        cut = slice(i * tile, (i + 1) * tile)
        g = grad[cut, :]
        wout[cut, :] = g.astype(jnp.bfloat16)
        prod = g * wch[c, cut, :].astype(jnp.float32)
        hi = prod.astype(jnp.bfloat16)
        lo = (prod - hi.astype(jnp.float32)).astype(jnp.bfloat16)
        sums = lax.dot_general(ones, hi, nt, preferred_element_type=jnp.float32)
        sums += lax.dot_general(ones, lo, nt, preferred_element_type=jnp.float32)
        gcols = pl.ds(pl.multiple_of(f * dn + i * tile, LANES), tile)
        gg[f, :, cut] = sums / gain[:, gcols]
    for o in range(1, nf):
        send(gg.at[f], gg.at[f], plan["gain"] + o, plan["gain"] + nf - o, {"fsdp": lax.rem(f + o, nf)})
    l_wout = local(7, wout, wgrad_h.at[0])

    for j in range(1, chips):
        for q in range(CHUNKS):
            rows = pl.ds(q * ct, ct)
            arrived(kp.at[j, rows, :], plan["kp"] + j * CHUNKS + q)
        kacc[...] += kp[j].astype(jnp.float32)
    kout[...] = kacc[...].astype(jnp.bfloat16)
    l_kout = local(8, kout, keys_h.at[0])

    for k in range(pieces):
        arrived(og.at[1 - h, k], plan["yag"] + k)
        l_og.append(local(10 + pieces + k, *outer_out(1 - h, k)))

    for o in range(1, nf):
        arrived(gg.at[lax.rem(f + o, nf)], plan["gain"] + o)
    for d in range(nf):
        gout[:, d * dn:(d + 1) * dn] = gg[d, 0:1, :]
    l_gout = local(9, gout, ggrad_h)

    for copy in sent:
        copy.wait_send()
    for copy in [l_wout, l_kout, l_gout] + l_og:
        copy.wait()


def exchange(nf, nr, token_ids, hidden, norm_gain, key_weight, key_cot, frag_base, frag_local):
    tok, d = hidden.shape[1:]
    dn, kw = frag_base.shape
    chips, outer = nf // CORES, nr // PAIR
    pieces = 4 if dn // 2 // outer % 16 == 0 else 2
    prows = dn * (kw // PAIR // LANES) // pieces
    plan, n_sem = semaphore_plan(nf, nr, pieces)
    bf, f32 = jnp.bfloat16, jnp.float32
    vmem = pltpu.VMEM
    anyspace = pl.BlockSpec(memory_space=pl.ANY)
    scratch = [
        vmem((1, tok), jnp.int32), vmem((tok, d), bf), vmem((1, d), f32), vmem((CORES, dn, kw), bf),
        vmem((tok, kw), bf), vmem((dn, kw), f32), vmem((dn, kw), bf),
        vmem((nf, tok, dn), bf), vmem((chips, CORES, tok, dn), bf), vmem((tok, dn), bf),
        vmem((chips, tok, dn), bf),
        vmem((tok, kw), bf), vmem((tok, kw), bf), vmem((chips, tok, kw), bf), vmem((chips, tok, kw), bf),
        vmem((chips, tok, kw), bf), vmem((chips, tok, kw), bf), vmem((tok, kw), f32), vmem((tok, kw), bf),
        vmem((dn, kw), f32), vmem((dn, kw), bf), vmem((nf, 8, dn), f32), vmem((1, d), f32),
        vmem((pieces, prows, LANES), bf), vmem((pieces, prows, LANES), bf), vmem((pieces, prows, LANES), bf),
        vmem((pieces, outer, prows // outer, LANES), bf), vmem((PAIR, pieces, prows, LANES), bf),
        pltpu.SemaphoreType.DMA((n_sem,)), pltpu.SemaphoreType.DMA((n_sem,)), pltpu.SemaphoreType.DMA((10 + 2 * pieces,)),
    ]
    return pl.pallas_call(
        functools.partial(kernel, nf, nr, pieces, plan),
        out_shape=(
            jax.ShapeDtypeStruct((1, tok, kw), bf),
            jax.ShapeDtypeStruct((1, dn, kw), bf),
            jax.ShapeDtypeStruct((1, d), f32),
            jax.ShapeDtypeStruct((dn, kw), bf),
        ),
        in_specs=[anyspace] * 7,
        out_specs=(anyspace,) * 4,
        scratch_shapes=scratch,
        compiler_params=pltpu.CompilerParams(
            collective_id=0, has_side_effects=True, vmem_limit_bytes=56 * 1024 * 1024
        ),
    )(token_ids, hidden, norm_gain, key_weight, key_cot, frag_base, frag_local)


def body(nf, nr, token_ids, hidden, norm_gain, key_weight, key_cot, frag_base, frag_local, momentum):
    keys, weight_grad, gain_grad, total = exchange(
        nf, nr, token_ids, hidden, norm_gain, key_weight, key_cot, frag_base, frag_local
    )
    outer_grad = total.astype(jnp.float32) / nr
    momentum_next = nesterov_mu * momentum.astype(jnp.float32) + outer_grad
    new_params = frag_base - outer_rate * (nesterov_mu * momentum_next + outer_grad)
    return (keys, weight_grad, gain_grad, new_params, momentum_next.astype(jnp.bfloat16))


def solution(mesh):
    return jax.shard_map(
        functools.partial(body, mesh.shape["fsdp"], mesh.shape["rep"]),
        mesh=mesh,
        in_specs=(
            P("rep", "fsdp"),
            P("rep", "fsdp", None),
            P("rep", None),
            P("rep", "fsdp", None),
            P("rep", "fsdp", None),
            P("fsdp", None),
            P("rep", "fsdp", None),
            P("fsdp", None),
        ),
        out_specs=(
            P("rep", "fsdp", None),
            P("rep", "fsdp", None),
            P("rep", None),
            P("fsdp", None),
            P("fsdp", None),
        ),
        check_vma=False,
    )
```

```python
import functools

import jax
import jax.numpy as jnp
from jax import lax
from jax.experimental import pallas as pl
from jax.experimental.pallas import tpu as pltpu
from jax.sharding import PartitionSpec as P

LEN = 64
LANES = 128
CORES = 2
PAIR = 2
CHUNKS = 4

pad_token = 128004
norm_eps = 1e-05
nesterov_mu = 0.9
outer_rate = 0.7

MESH = pl.DeviceIdType.MESH


class Counter:
    def __init__(self):
        self.n = 0

    def take(self, count=1):
        first = self.n
        self.n += count
        return first


def semaphore_plan(nf, nr, pieces):
    chips, outer = nf // CORES, nr // PAIR
    c = Counter()
    plan = {
        "w": c.take(),
        "sib": c.take(),
        "wt_sib": c.take(),
        "wt": c.take(chips),
        "wt_fwd": c.take(chips),
        "nrm": c.take(chips * CHUNKS),
        "fwd": c.take(chips * CHUNKS),
        "kp": c.take(chips * CHUNKS),
        "gain": c.take(nf),
        "y": c.take(pieces),
        "z": c.take(pieces * outer),
        "zag": c.take(pieces * outer),
        "yag": c.take(pieces),
    }
    return plan, c.n


def transposed_dot(a, b):
    return lax.dot_general(a, b, (((0,), (0,)), ((), ())), preferred_element_type=jnp.float32)


def kernel(
    nf, nr, pieces, plan,
    ids_h, hid_h, gain_h, w_h, cot_h, base_h, loc_h,
    keys_h, wgrad_h, ggrad_h, outer_h,
    ids, hid, gain, wch, cot, base, loc,
    nrm, rn, sn, fn, wt, wt_s, wt_p, wt_f, pk, kp, kacc, kout,
    grad, wout, gg, gout,
    ps, yr, ys, zr, og,
    ss, rs, ls,
):
    tok = hid.shape[0]
    dn = base.shape[0]
    chips, outer = nf // CORES, nr // PAIR
    width = base.shape[1] // PAIR
    groups = width // LANES
    prows = dn * groups // pieces
    zrows = prows // outer
    unit = tok // 16
    edges = [0, 4 * unit, 9 * unit, 14 * unit, tok]
    spans = [pl.ds(a, b - a) for a, b in zip(edges[:-1], edges[1:])]
    early, late = slice(0, edges[2]), slice(edges[2], tok)
    f = lax.axis_index("fsdp")
    r = lax.axis_index("rep")
    x, c = lax.div(f, CORES), lax.rem(f, CORES)
    sib = f + 1 - 2 * c
    z, h = lax.div(r, PAIR), lax.rem(r, PAIR)
    partner = r + 1 - 2 * h

    def chip_at(j):
        return lax.rem(x + j, chips)

    def z_at(j):
        return lax.rem(z + j, outer)

    def local(i, src, dst):
        copy = pltpu.make_async_copy(src, dst, ls.at[i])
        copy.start()
        return copy

    l_gain = local(2, gain_h, gain)
    l_hid = []
    for q, rows in enumerate(spans):
        l_hid.append(local(10 + 4 * pieces + q, hid_h.at[0, rows, :], hid.at[rows, :]))
        if q == 0:
            l_base = local(5, base_h, base)
            l_loc = local(6, loc_h.at[0], loc)
            l_ids = local(1, ids_h, ids)
            l_cot = local(0, cot_h.at[0], cot)
    l_w = local(4, w_h.at[0], wch.at[c])

    barrier = pltpu.get_barrier_semaphore()
    greeted = 0
    for o in range(1, nf):
        pl.semaphore_signal(barrier, inc=1, device_id={"fsdp": lax.rem(f + o, nf)}, device_id_type=MESH)
        greeted += 1
    pl.semaphore_signal(barrier, inc=1, device_id={"rep": partner}, device_id_type=MESH)
    greeted += 1
    for o in range(1, outer):
        pl.semaphore_signal(barrier, inc=1, device_id={"rep": z_at(o) * PAIR + h}, device_id_type=MESH)
        greeted += 1

    sent = []

    def copy_of(src, dst, sid, rid, dev):
        return pltpu.make_async_remote_copy(
            src_ref=src, dst_ref=dst, send_sem=ss.at[sid], recv_sem=rs.at[rid],
            device_id=dev, device_id_type=MESH,
        )

    def send(src, dst, sid, rid, dev):
        copy = copy_of(src, dst, sid, rid, dev)
        copy.start()
        sent.append(copy)

    def arrived(dst, rid):
        copy_of(dst, dst, rid, rid, {"fsdp": sib}).wait_recv()

    def peer(j):
        return {"fsdp": chip_at(j) * CORES + c}

    l_gain.wait()
    sub = 16

    def norm_rows(i, carry):
        rows = pl.ds(pl.multiple_of(i * sub, sub), sub)
        v = hid[rows, :].astype(jnp.float32)
        inv = lax.rsqrt(jnp.mean(v * v, -1, keepdims=True) + norm_eps)
        for d in range(nf):
            part = hid[rows, d * dn:(d + 1) * dn].astype(jnp.float32)
            nrm[d, rows, :] = (part * inv * gain[:, d * dn:(d + 1) * dn]).astype(jnp.bfloat16)
        return carry

    def norm_chunk(q):
        l_hid[q].wait()
        lax.fori_loop(edges[q] // sub, edges[q + 1] // sub, norm_rows, 0)
        if q == 0:
            pl.semaphore_wait(barrier, greeted)
        rows = spans[q]
        for j in range(1, chips):
            send(
                nrm.at[pl.ds(chip_at(j) * CORES, CORES), rows, :],
                rn.at[chips - j, :, rows, :],
                plan["nrm"] + j * CHUNKS + q,
                plan["nrm"] + (chips - j) * CHUNKS + q,
                peer(j),
            )

    norm_chunk(0)

    step = min(64, prows)

    def pseudo(half, k, rows):
        g, b = k % groups, k // groups
        cols = pl.ds(pl.multiple_of(half * width + g * LANES, LANES), LANES)
        rows = pl.ds(pl.multiple_of(b * prows + rows * step, step), step)
        return (base[rows, cols] - loc[rows, cols].astype(jnp.float32)).astype(jnp.bfloat16)

    def pseudo_rows(k, i, carry):
        ps[k, pl.ds(pl.multiple_of(i * step, step), step), :] = pseudo(1 - h, k, i)
        return carry

    l_base.wait()
    l_loc.wait()
    for k in range(pieces):
        lax.fori_loop(0, prows // step, functools.partial(pseudo_rows, k), 0)
        send(ps.at[k], yr.at[k], plan["y"] + k, plan["y"] + k, {"rep": partner})

    norm_chunk(1)
    send(w_h.at[0], wch.at[c], plan["w"], plan["w"], {"fsdp": sib})

    l_ids.wait()
    row = lax.broadcasted_iota(jnp.int32, (tok, tok), 0)
    col = lax.broadcasted_iota(jnp.int32, (tok, tok), 1)
    live = jnp.where(ids[...] != pad_token, 1.0, 0.0).astype(jnp.float32)
    live = jnp.broadcast_to(live, (tok, tok))
    count = jnp.sum(jnp.where(lax.div(row, LEN) == lax.div(col, LEN), live, 0.0), -1, keepdims=True)
    own = jnp.sum(jnp.where(row == col, live, 0.0), -1, keepdims=True)
    loss_weight = LEN * own / count
    l_cot.wait()
    wt[...] = (loss_weight * cot[...].astype(jnp.float32)).astype(jnp.bfloat16)

    for j in range(1, chips):
        send(wt, wt_p.at[chips - j], plan["wt"] + j, plan["wt"] + chips - j, peer(j))
    send(wt, wt_s, plan["wt_sib"], plan["wt_sib"], {"fsdp": sib})

    tile = min(256, dn)

    def grad_tiles(rows_of, weighted, first):
        for i in range(dn // tile):
            cut = slice(i * tile, (i + 1) * tile)
            term = transposed_dot(rows_of(cut), weighted())
            if first:
                grad[cut, :] = term
            else:
                grad[cut, :] += term

    def peer_chunk(q):
        rows = spans[q]
        for j in range(1, chips):
            if q == 1:
                arrived(wt_p.at[j], plan["wt"] + j)
                send(wt_p.at[j], wt_f.at[j], plan["wt_fwd"] + j, plan["wt_fwd"] + j, {"fsdp": sib})
            arrived(rn.at[j, :, rows, :], plan["nrm"] + j * CHUNKS + q)
            send(
                rn.at[j, 1 - c, rows, :], fn.at[j, rows, :],
                plan["fwd"] + j * CHUNKS + q, plan["fwd"] + j * CHUNKS + q, {"fsdp": sib},
            )
            part = jnp.dot(rn[j, 0, rows, :], wch[0], preferred_element_type=jnp.float32)
            part += jnp.dot(rn[j, 1, rows, :], wch[1], preferred_element_type=jnp.float32)
            pk[j, rows, :] = part.astype(jnp.bfloat16)
            send(
                pk.at[j, rows, :], kp.at[chips - j, rows, :],
                plan["kp"] + j * CHUNKS + q, plan["kp"] + (chips - j) * CHUNKS + q, peer(j),
            )

    def own_keys(half):
        n = tok // 2
        rows = slice(half * n, (half + 1) * n)
        kacc[rows, :] = jnp.dot(nrm[2 * x, rows, :], wch[0], preferred_element_type=jnp.float32)
        kacc[rows, :] += jnp.dot(nrm[2 * x + 1, rows, :], wch[1], preferred_element_type=jnp.float32)

    def pair_sum(k):
        arrived(yr.at[k], plan["y"] + k)

        def some(i, carry):
            rows = pl.ds(pl.multiple_of(i * step, step), step)
            total = pseudo(h, k, i).astype(jnp.float32) + yr[k, rows, :].astype(jnp.float32)
            ys[k, rows, :] = total.astype(jnp.bfloat16)
            return carry

        lax.fori_loop(0, prows // step, some, 0)
        for o in range(1, outer):
            send(
                ys.at[k, pl.ds(pl.multiple_of(z_at(o) * zrows, 16), zrows), :],
                zr.at[k, outer - o],
                plan["z"] + k * outer + o, plan["z"] + k * outer + outer - o,
                {"rep": z_at(o) * PAIR + h},
            )

    mine = pl.ds(pl.multiple_of(z * zrows, 16), zrows)

    def outer_sum(k):
        total = ys[k, mine, :].astype(jnp.float32)
        for o in range(1, outer):
            arrived(zr.at[k, o], plan["z"] + k * outer + o)
            total += zr[k, o].astype(jnp.float32)
        og[h, k, mine, :] = total.astype(jnp.bfloat16)
        for o in range(1, outer):
            send(
                og.at[h, k, mine, :], og.at[h, k, mine, :],
                plan["zag"] + k * outer + o, plan["zag"] + k * outer + outer - o,
                {"rep": z_at(o) * PAIR + h},
            )

    l_og = []

    def outer_back(k):
        for o in range(1, outer):
            there = pl.ds(pl.multiple_of(z_at(o) * zrows, 16), zrows)
            arrived(og.at[h, k, there, :], plan["zag"] + k * outer + o)
        send(og.at[h, k], og.at[h, k], plan["yag"] + k, plan["yag"] + k, {"rep": partner})

    def outer_out(half, k, slot):
        g, b = k % groups, k // groups
        cols = pl.ds(pl.multiple_of(half * width + g * LANES, LANES), LANES)
        l_og.append(local(10 + slot, og.at[half, k], outer_h.at[pl.ds(b * prows, prows), cols]))

    def pair_back(k):
        arrived(og.at[1 - h, k], plan["yag"] + k)
        outer_out(1 - h, k, pieces + k)

    def piece(step_of, k):
        if k < pieces:
            step_of(k)

    pair_sum(0)
    norm_chunk(2)
    pair_sum(1)
    norm_chunk(3)
    send(nrm.at[sib], sn, plan["sib"], plan["sib"], {"fsdp": sib})
    outer_sum(0)
    piece(pair_sum, 2)
    outer_sum(1)
    piece(pair_sum, 3)
    l_w.wait()
    arrived(wch.at[1 - c], plan["w"])
    peer_chunk(0)
    outer_back(0)
    piece(outer_sum, 2)
    own_keys(0)
    outer_back(1)
    piece(outer_sum, 3)
    own_keys(1)
    peer_chunk(1)
    piece(outer_back, 2)
    grad_tiles(lambda cut: nrm[f, :, cut], lambda: wt[...], True)
    piece(outer_back, 3)
    for k in range(pieces):
        outer_out(h, k, k)
    arrived(wt_s, plan["wt_sib"])
    arrived(sn, plan["sib"])
    grad_tiles(lambda cut: sn[:, cut], lambda: wt_s[...], False)
    for j in range(1, chips):
        grad_tiles(lambda cut: rn[j, c, early, cut], lambda: wt_p[j, early, :], False)
        arrived(wt_f.at[j], plan["wt_fwd"] + j)
        for q in range(2):
            arrived(fn.at[j, spans[q], :], plan["fwd"] + j * CHUNKS + q)
        grad_tiles(lambda cut: fn[j, early, cut], lambda: wt_f[j, early, :], False)
    peer_chunk(2)
    peer_chunk(3)

    for j in range(1, chips):
        for q in range(2, CHUNKS):
            arrived(fn.at[j, spans[q], :], plan["fwd"] + j * CHUNKS + q)
    ones = jnp.ones((8, wout.shape[1]), jnp.bfloat16)
    nt = (((1,), (1,)), ((), ()))
    for i in range(dn // tile):
        cut = slice(i * tile, (i + 1) * tile)
        g = grad[cut, :]
        for j in range(1, chips):
            g += transposed_dot(rn[j, c, late, cut], wt_p[j, late, :])
            g += transposed_dot(fn[j, late, cut], wt_f[j, late, :])
        wout[cut, :] = g.astype(jnp.bfloat16)
        prod = g * wch[c, cut, :].astype(jnp.float32)
        hi = prod.astype(jnp.bfloat16)
        lo = (prod - hi.astype(jnp.float32)).astype(jnp.bfloat16)
        sums = lax.dot_general(ones, hi, nt, preferred_element_type=jnp.float32)
        sums += lax.dot_general(ones, lo, nt, preferred_element_type=jnp.float32)
        gcols = pl.ds(pl.multiple_of(f * dn + i * tile, LANES), tile)
        gg[f, :, cut] = sums / gain[:, gcols]
    for o in range(1, nf):
        send(gg.at[f], gg.at[f], plan["gain"] + o, plan["gain"] + nf - o, {"fsdp": lax.rem(f + o, nf)})
    l_wout = local(7, wout, wgrad_h.at[0])

    for j in range(1, chips):
        for q in range(CHUNKS):
            rows = spans[q]
            arrived(kp.at[j, rows, :], plan["kp"] + j * CHUNKS + q)
        kacc[...] += kp[j].astype(jnp.float32)
    kout[...] = kacc[...].astype(jnp.bfloat16)
    l_kout = local(8, kout, keys_h.at[0])

    for k in range(pieces):
        pair_back(k)

    for o in range(1, nf):
        arrived(gg.at[lax.rem(f + o, nf)], plan["gain"] + o)
    for d in range(nf):
        gout[:, d * dn:(d + 1) * dn] = gg[d, 0:1, :]
    l_gout = local(9, gout, ggrad_h)

    for copy in sent:
        copy.wait_send()
    for copy in [l_wout, l_kout, l_gout] + l_og:
        copy.wait()


def exchange(nf, nr, token_ids, hidden, norm_gain, key_weight, key_cot, frag_base, frag_local):
    tok, d = hidden.shape[1:]
    dn, kw = frag_base.shape
    chips, outer = nf // CORES, nr // PAIR
    pieces = 4 if dn // 2 // outer % 16 == 0 else 2
    prows = dn * (kw // PAIR // LANES) // pieces
    plan, n_sem = semaphore_plan(nf, nr, pieces)
    bf, f32 = jnp.bfloat16, jnp.float32
    vmem = pltpu.VMEM
    anyspace = pl.BlockSpec(memory_space=pl.ANY)
    scratch = [
        vmem((1, tok), jnp.int32), vmem((tok, d), bf), vmem((1, d), f32), vmem((CORES, dn, kw), bf),
        vmem((tok, kw), bf), vmem((dn, kw), f32), vmem((dn, kw), bf),
        vmem((nf, tok, dn), bf), vmem((chips, CORES, tok, dn), bf), vmem((tok, dn), bf),
        vmem((chips, tok, dn), bf),
        vmem((tok, kw), bf), vmem((tok, kw), bf), vmem((chips, tok, kw), bf), vmem((chips, tok, kw), bf),
        vmem((chips, tok, kw), bf), vmem((chips, tok, kw), bf), vmem((tok, kw), f32), vmem((tok, kw), bf),
        vmem((dn, kw), f32), vmem((dn, kw), bf), vmem((nf, 8, dn), f32), vmem((1, d), f32),
        vmem((pieces, prows, LANES), bf), vmem((pieces, prows, LANES), bf), vmem((pieces, prows, LANES), bf),
        vmem((pieces, outer, prows // outer, LANES), bf), vmem((PAIR, pieces, prows, LANES), bf),
        pltpu.SemaphoreType.DMA((n_sem,)), pltpu.SemaphoreType.DMA((n_sem,)), pltpu.SemaphoreType.DMA((10 + 4 * pieces + CHUNKS,)),
    ]
    return pl.pallas_call(
        functools.partial(kernel, nf, nr, pieces, plan),
        out_shape=(
            jax.ShapeDtypeStruct((1, tok, kw), bf),
            jax.ShapeDtypeStruct((1, dn, kw), bf),
            jax.ShapeDtypeStruct((1, d), f32),
            jax.ShapeDtypeStruct((dn, kw), bf),
        ),
        in_specs=[anyspace] * 7,
        out_specs=(anyspace,) * 4,
        scratch_shapes=scratch,
        compiler_params=pltpu.CompilerParams(
            collective_id=0, has_side_effects=True, vmem_limit_bytes=56 * 1024 * 1024
        ),
    )(token_ids, hidden, norm_gain, key_weight, key_cot, frag_base, frag_local)


def body(nf, nr, token_ids, hidden, norm_gain, key_weight, key_cot, frag_base, frag_local, momentum):
    keys, weight_grad, gain_grad, total = exchange(
        nf, nr, token_ids, hidden, norm_gain, key_weight, key_cot, frag_base, frag_local
    )
    outer_grad = total.astype(jnp.float32) / nr
    momentum_next = nesterov_mu * momentum.astype(jnp.float32) + outer_grad
    new_params = frag_base - outer_rate * (nesterov_mu * momentum_next + outer_grad)
    return (keys, weight_grad, gain_grad, new_params, momentum_next.astype(jnp.bfloat16))


def solution(mesh):
    return jax.shard_map(
        functools.partial(body, mesh.shape["fsdp"], mesh.shape["rep"]),
        mesh=mesh,
        in_specs=(
            P("rep", "fsdp"),
            P("rep", "fsdp", None),
            P("rep", None),
            P("rep", "fsdp", None),
            P("rep", "fsdp", None),
            P("fsdp", None),
            P("rep", "fsdp", None),
            P("fsdp", None),
        ),
        out_specs=(
            P("rep", "fsdp", None),
            P("rep", "fsdp", None),
            P("rep", None),
            P("fsdp", None),
            P("fsdp", None),
        ),
        check_vma=False,
    )
```
